256 devices in a mesh: vocab: 4 (over y), hidden: 64 (over x, z, core).
Axes of the slice: x: 4, y: 4, z: 8, core: 2. Of those that a mesh axis runs over, the one named last changes fastest.
Arguments:
- gradient: bfloat16 [1024, 14336], P('vocab', 'hidden'), may hold values from -6 to 6
- moment_first: float32 [4096, 14336], P('vocab', 'hidden'), may hold values from -6 to 6
- moment_second: float32 [4096, 14336], P('vocab', 'hidden'), may hold values from 0.05 to 2
- basis: bfloat16 [14336, 14336], P('hidden'), may hold values from -0.125 to 0.125
- block_ids: int32 [4, 2], replicated, may hold values from -1 to 7, as said below
Outputs:
- update: float32 [1024, 14336], P('vocab', 'hidden')
- new_first: float32 [4096, 14336], P('vocab', 'hidden')
- new_second: float32 [4096, 14336], P('vocab', 'hidden')
The draws below stay inside these ranges and needn't reach their ends.
Inputs may be any that keep to these rules, and one draw needn't show every extreme that they name: `block_ids`: live slots in all number 4; one or two owners have 2 live slots, the same number of owners have none, and every other owner has one; an owner's live slots are its first ones, and its live entries are distinct resident blocks of that owner.
All inputs are finite; a program needn't handle non-finite values.
Results may differ from the reference program's by a relative error of at most 0.0029.
Values may be sent and summed in bfloat16 or wider, within the bound.
No kernel may reach another device: no remote copies, remote signals or barrier semaphores. Data moves between devices by JAX's collectives and lax.ppermute only.
A program may use at most 64 MiB of HBM per device.

```python
import math
import jax
import jax.numpy as jnp
from jax import lax

D = 14336
BLK = 128
CAP = 2
TBL = 8
OWNERS = 4
SLOT_ROWS = 1024
TABLE_ROWS = 4096


def draw_block_ids(key, part):
    key = jax.random.fold_in(key, 41)
    key_order, key_count, key_blocks, key_special = jax.random.split(key, 4)
    order = jax.random.permutation(key_order, OWNERS)
    doubled = jax.random.randint(key_count, (), 1, OWNERS // 2 + 1)
    ranks = jnp.arange(OWNERS)
    values = jnp.where(ranks < doubled, CAP, jnp.where(ranks < 2 * doubled, 0, 1)).astype(jnp.int32)
    counts = jnp.zeros((OWNERS,), jnp.int32).at[order].set(values)
    subkeys = jax.random.split(key_blocks, OWNERS)
    chosen = jax.vmap(lambda subkey: jax.random.permutation(subkey, TBL)[:CAP])(subkeys)
    pick = jax.random.randint(key_special, (), 0, OWNERS // 2 + 1)
    special = order[jnp.minimum(pick, doubled - 1)]
    highest = TBL - 1 - jnp.arange(CAP)
    picked = jnp.where((jnp.arange(OWNERS) == special)[:, None], highest[None, :], chosen)
    live = jnp.arange(CAP)[None, :] < counts[:, None]
    return jnp.where(live, picked, -1).astype(jnp.int32)


def strengthened(entries, stream_key, source, target, parts, factor):
    def block_of(axis_at):
        return (jnp.arange(entries.shape[axis_at]) // (entries.shape[axis_at] // parts)).reshape((-1,) + (1,) * (entries.ndim - 1 - axis_at))

    first = jax.random.permutation(stream_key, parts)[block_of(target)]
    far = (block_of(target) + parts // 2) % parts
    return jnp.where((block_of(source) == first) | (block_of(source) == far), factor * entries, entries)


def block_levels(stream_key, dims, cuts, smallest, largest):
    loudness = 1.0
    for dim, shards_of in cuts:
        heights = jax.random.uniform(jax.random.fold_in(jax.random.fold_in(stream_key, 6), dim), (shards_of,), jnp.float32, smallest / len(cuts), largest / len(cuts))
        loudness = loudness * jnp.repeat(jnp.exp(heights), dims[dim] // shards_of).reshape((-1,) + (1,) * (len(dims) - 1 - dim))
    return loudness


def bell_draw(rng, shape, scale, limit, cuts=(), kind=jnp.bfloat16):
    factor_of = block_levels(rng, shape, cuts, -0.22, 0.18) if cuts else 1.0
    drawn = jax.random.normal(rng, shape, jnp.float32) * scale * factor_of
    return jnp.minimum(jnp.maximum(drawn, -limit), limit).astype(kind)


def gaussian_with(key, dims, width, reach, shards, heavy, held_as=jnp.bfloat16):
    array = width * jax.random.normal(key, dims, jnp.float32)
    if shards:
        array = array * block_levels(key, dims, shards, -0.22, 0.18)
    return jnp.clip(strengthened(array, jax.random.fold_in(key, 3), *heavy), -reach, reach).astype(held_as)


def setup_inputs(seed: int = 0) -> dict:
    arg_keys = jax.random.split(jax.random.key(seed), 6)
    gradient = bell_draw(arg_keys[0], (SLOT_ROWS, D), 1.0, 6.0, ((0, 4), (1, 64)))
    moment_first = bell_draw(arg_keys[1], (TABLE_ROWS, D), 1.0, 6.0, ((0, 4), (1, 64)), jnp.float32)
    moment_second = jnp.clip(jnp.exp(math.log(2.0) - 3.6888794 * jax.random.uniform(arg_keys[2], (TABLE_ROWS, D), jnp.float32) ** block_levels(arg_keys[2], (TABLE_ROWS, D), ((0, 4), (1, 64)), -0.2, 0.2)), 0.05, 2.0)
    basis = gaussian_with(arg_keys[3], (D, D), D ** -0.5, 0.125, ((0, 64),), (0, 1, 64, 4.0))
    block_ids = draw_block_ids(jax.random.fold_in(arg_keys[5], 71), 0)
    return dict(gradient=gradient, moment_first=moment_first, moment_second=moment_second, basis=basis, block_ids=block_ids)


beta_first = 0.9
beta_second = 0.95
epsilon = 1e-08

def reference(gradient, moment_first, moment_second, basis, block_ids):
    whole_basis = basis.astype(jnp.float32)
    grad_blocks = gradient.reshape(OWNERS, CAP, BLK, D)
    first_table = moment_first.reshape(OWNERS, TBL, BLK, D)
    second_table = moment_second.reshape(OWNERS, TBL, BLK, D)
    block_counts = lax.optimization_barrier(jnp.sum((block_ids >= 0).astype(jnp.int32), axis=1)).astype(jnp.int32)
    block_ends = jnp.cumsum(block_counts).astype(jnp.int32)
    block_starts = (block_ends - block_counts).astype(jnp.int32)
    compact = jnp.arange(OWNERS, dtype=jnp.int32)
    holder = lax.optimization_barrier(jnp.sum((block_ends[None, :] <= compact[:, None]).astype(jnp.int32), axis=1)).astype(jnp.int32)
    slot_index = (compact - block_starts[holder]).astype(jnp.int32)
    resident = block_ids[holder, slot_index]
    chosen = grad_blocks[holder, slot_index].reshape(OWNERS * BLK, D).astype(jnp.float32)
    rotated = jnp.dot(chosen, whole_basis, precision=lax.Precision.HIGHEST)
    old_first = first_table[holder, resident].reshape(OWNERS * BLK, D)
    old_second = second_table[holder, resident].reshape(OWNERS * BLK, D)
    first = beta_first * old_first + (1.0 - beta_first) * rotated
    second = beta_second * old_second + (1.0 - beta_second) * rotated * rotated
    direction = (first / (jnp.sqrt(second) + epsilon)).astype(jnp.bfloat16)
    update_rows = jnp.dot(direction.astype(jnp.float32), whole_basis.T, precision=lax.Precision.HIGHEST)
    update = jnp.zeros((OWNERS, CAP, BLK, D), jnp.float32)
    update = update.at[holder, slot_index].set(update_rows.reshape(OWNERS, BLK, D))
    new_first = first_table.at[holder, resident].set(first.reshape(OWNERS, BLK, D))
    new_second = second_table.at[holder, resident].set(second.reshape(OWNERS, BLK, D))
    return (update.reshape(SLOT_ROWS, D), new_first.reshape(TABLE_ROWS, D), new_second.reshape(TABLE_ROWS, D))
```

```python
import functools

import jax
import jax.numpy as jnp
from jax import lax
from jax.experimental import pallas as pl
from jax.experimental.pallas import tpu as pltpu
from jax.sharding import Mesh
from jax.sharding import PartitionSpec as P

BLK = 128
OWNERS = 4
XS, ZH, ZL, CORES = 4, 4, 2, 2
SCALE = 4.0

beta_first = 0.9
beta_second = 0.95
epsilon = 1e-08

f32, bf16, f16 = jnp.float32, jnp.bfloat16, jnp.float16


def rotate_kernel(core_ref, basis_ref, rows_ref, keep_ref, send_ref):
    width = rows_ref.shape[1]
    part = lax.dot_general(
        basis_ref[...], rows_ref[...], (((0,), (1,)), ((), ())), preferred_element_type=f32
    )
    part = part.reshape(ZL, CORES, width, BLK) * SCALE
    mine = core_ref[0] == 0
    keep_ref[0, :, 0] = jnp.where(mine, part[:, 0], part[:, 1])
    send_ref[0, :, 0] = jnp.where(mine, part[:, 1], part[:, 0])


def rotate_partials(core, basis, rows):
    width = rows.shape[1]
    cols = ZL * CORES * width
    shape = (XS, ZL, ZH, width, BLK)
    out = pl.BlockSpec((1, ZL, 1, width, BLK), lambda i: (i // ZH, 0, i % ZH, 0, 0))
    return pl.pallas_call(
        rotate_kernel,
        grid=(XS * ZH,),
        in_specs=[
            pl.BlockSpec(memory_space=pltpu.SMEM),
            pl.BlockSpec((width, cols), lambda i: (0, i)),
            pl.BlockSpec((BLK, width), lambda i: (0, 0)),
        ],
        out_specs=[out, out],
        out_shape=[jax.ShapeDtypeStruct(shape, f32)] * 2,
    )(core, basis, rows)


def back_kernel(core_ref, basis_ref, own_ref, other_ref, out_ref):
    width = basis_ref.shape[0]
    own = own_ref[0, :, 0]
    other = other_ref[0, :, 0]
    mine = core_ref[0] == 0
    even = jnp.where(mine, own, other)
    odd = jnp.where(mine, other, own)
    cols = jnp.stack([even, odd], axis=1).reshape(ZL * CORES * width, BLK)
    part = jnp.dot(basis_ref[...], cols, preferred_element_type=f32)

    @pl.when(pl.program_id(0) == 0)
    def _():
        out_ref[...] = part

    @pl.when(pl.program_id(0) > 0)
    def _():
        out_ref[...] += part


def rotate_back(core, basis, own, other):
    width = own.shape[3]
    cols = ZL * CORES * width
    block = pl.BlockSpec((1, ZL, 1, width, BLK), lambda i: (i // ZH, 0, i % ZH, 0, 0))
    return pl.pallas_call(
        back_kernel,
        grid=(XS * ZH,),
        in_specs=[
            pl.BlockSpec(memory_space=pltpu.SMEM),
            pl.BlockSpec((width, cols), lambda i: (0, i)),
            block,
            block,
        ],
        out_specs=pl.BlockSpec((width, BLK), lambda i: (0, 0)),
        out_shape=jax.ShapeDtypeStruct((width, BLK), f32),
    )(core, basis, own, other)


def adam_moments(rotated, old_first, old_second):
    first = beta_first * old_first + (1.0 - beta_first) * rotated
    second = beta_second * old_second + (1.0 - beta_second) * rotated * rotated
    direction = (first / (jnp.sqrt(second) + epsilon)).astype(bf16)
    return (first, second, direction)


def from_owner(x, distance):
    got = [
        lax.ppermute(x, "y", [(i, (i + k) % OWNERS) for i in range(OWNERS)])
        for k in range(1, OWNERS)
    ]
    out = got[0]
    for k in range(2, OWNERS):
        out = jnp.where(distance == k, got[k - 1], out)
    return out


def all_to_all(x, axes):
    return lax.all_to_all(x, axes, 0, 0, tiled=True)


def swap_cores(x):
    return lax.ppermute(x, "c", [(0, 1), (1, 0)])


def shards(gradient, moment_first, moment_second, basis, block_ids):
    width = gradient.shape[1]
    table_blocks = moment_first.shape[0] // BLK
    me = lax.axis_index("y")
    core = lax.axis_index("c").astype(jnp.int32).reshape(1)

    counts = jnp.sum((block_ids >= 0).astype(jnp.int32), axis=1)
    full, empty = counts == 2, counts == 0
    full_rank = jnp.cumsum(full.astype(jnp.int32))
    empty_rank = jnp.cumsum(empty.astype(jnp.int32))
    owners = jnp.arange(OWNERS, dtype=jnp.int32)
    count = counts[me]
    source = jnp.sum(jnp.where(full & (full_rank == empty_rank[me]), owners, 0))
    helper = jnp.sum(jnp.where(empty & (empty_rank == full_rank[me]), owners, 0))
    back_to_source = (me - source) % OWNERS
    back_to_helper = (me - helper) % OWNERS
    helping = count == 0
    doubled = count == 2

    ids = jnp.clip(block_ids[me], 0, table_blocks - 1)
    first_table = moment_first.reshape(table_blocks, BLK, width)
    second_table = moment_second.reshape(table_blocks, BLK, width)
    old_first = first_table[ids]
    old_second = second_table[ids]

    rows = jnp.where(helping, from_owner(gradient[BLK:], back_to_source), gradient[:BLK])
    lent_first = from_owner(old_first[1], back_to_source)
    lent_second = from_owner(old_second[1], back_to_source)
    work_first = jnp.where(helping, lent_first, old_first[0])
    work_second = jnp.where(helping, lent_second, old_second[0])

    keep, send = rotate_partials(core, basis, rows)
    part = (keep + swap_cores(send.astype(f16)).astype(f32)).astype(f16)
    part = all_to_all(part.reshape(XS * ZL, ZH * width, BLK), ("x", "zl"))
    part = jnp.sum(part.astype(f32), axis=0).astype(f16)
    part = all_to_all(part.reshape(ZH, width, BLK), "zh")
    rotated = (jnp.sum(part.astype(f32), axis=0) * (1.0 / SCALE)).T

    first, second, direction = adam_moments(rotated, work_first, work_second)
    gathered = jnp.broadcast_to(direction.T[None], (ZH, width, BLK))
    gathered = all_to_all(gathered, "zh")
    gathered = jnp.broadcast_to(gathered[None], (XS * ZL, ZH, width, BLK))
    gathered = all_to_all(gathered, ("x", "zl")).reshape(XS, ZL, ZH, width, BLK)

    other_rotated = from_owner(rotated, back_to_helper)
    first_1, second_1, _ = adam_moments(other_rotated, old_first[1], old_second[1])
    block = jnp.arange(table_blocks)
    zero_at = jnp.where(count >= 1, ids[0], -1)
    one_at = jnp.where(doubled, ids[1], -1)

    def written(table, zero, one):
        out = jnp.where((block == zero_at)[:, None, None], zero[None], table)
        out = jnp.where((block == one_at)[:, None, None], one[None], out)
        return out.reshape(table_blocks * BLK, width)

    new_first = written(first_table, first, first_1)
    new_second = written(second_table, second, second_1)

    update = rotate_back(core, basis, gathered, swap_cores(gathered)).T
    lent = from_owner(update.astype(f16), back_to_helper).astype(f32)
    update = jnp.concatenate(
        [jnp.where(count >= 1, update, 0.0), jnp.where(doubled, lent, 0.0)], axis=0
    )
    return (update, new_first, new_second)


def solution(mesh):
    split = Mesh(
        mesh.devices.reshape(OWNERS, XS, ZH, ZL, CORES), ("y", "x", "zh", "zl", "c")
    )
    hidden = ("x", "zh", "zl", "c")
    placed = (P("y", hidden), P("y", hidden), P("y", hidden), P(hidden, None), P())
    return jax.shard_map(
        shards,
        mesh=split,
        in_specs=placed,
        out_specs=(P("y", hidden),) * 3,
        check_vma=False,
    )
```

```python
import functools

import jax
import jax.numpy as jnp
from jax import lax
from jax.experimental import pallas as pl
from jax.experimental.pallas import tpu as pltpu
from jax.sharding import PartitionSpec as P

BLK = 128
OWNERS = 4
XS, ZS, CORES = 4, 8, 2
HIDDEN = XS * ZS * CORES
NEAR, FAR = 4, 8
SCALE = 4.0
VMEM_LIMIT = 32 * 2**20
NEAR_LIMIT = 32 * 2**20

beta_first = 0.9
beta_second = 0.95
epsilon = 1e-08

f32, bf16, f16 = jnp.float32, jnp.bfloat16, jnp.float16

smem = pl.BlockSpec(memory_space=pltpu.SMEM)
vmem = pl.BlockSpec(memory_space=pltpu.VMEM)
anywhere = pl.BlockSpec(memory_space=pl.ANY)
params = pltpu.CompilerParams(vmem_limit_bytes=VMEM_LIMIT)

MATCH, COUNT, ID_0, ID_1 = range(4)


def live_slots(ids_ref, owner):
    return (ids_ref[0, owner] >= 0).astype(jnp.int32) + (ids_ref[1, owner] >= 0).astype(jnp.int32)


def matching(ids_ref):
    zero = live_slots(ids_ref, 0)
    return jnp.where(
        zero + live_slots(ids_ref, 1) == 2,
        1,
        jnp.where(zero + live_slots(ids_ref, 2) == 2, 2, 3),
    )


def pick(match, options):
    return jnp.where(match == 1, options[0], jnp.where(match == 2, options[1], options[2]))


def near_kernel(basis_ref, out_ref, sem):
    copy = pltpu.make_async_copy(basis_ref, out_ref, sem)
    copy.start()
    copy.wait()


def brought_near(basis):
    return pl.pallas_call(
        near_kernel,
        in_specs=[anywhere],
        out_specs=vmem,
        out_shape=jax.ShapeDtypeStruct(basis.shape, basis.dtype),
        scratch_shapes=[pltpu.SemaphoreType.DMA],
        compiler_params=pltpu.CompilerParams(vmem_limit_bytes=NEAR_LIMIT),
    )(basis)


def rotate_kernel(
    ids_ref, basis_ref, own_ref, one_ref, two_ref, three_ref, keep_ref, send_ref, roles_ref
):
    width = own_ref.shape[0]
    cols = 2 * CORES * width
    me = lax.axis_index("vocab")
    match, count = matching(ids_ref), live_slots(ids_ref, me)
    roles_ref[MATCH], roles_ref[COUNT] = match, count
    roles_ref[ID_0], roles_ref[ID_1] = ids_ref[0, me], ids_ref[1, me]
    lent = pick(match, [one_ref[...], two_ref[...], three_ref[...]])
    rows = jnp.where(count == 0, lent, own_ref[...]) * jnp.bfloat16(SCALE)
    mine = lax.rem(lax.axis_index("hidden"), CORES) == 0

    for i in range(XS * ZS // 2):
        at = pl.ds(i * cols, cols)
        part = lax.dot_general(
            basis_ref[:, at], rows, (((0,), (0,)), ((), ())), preferred_element_type=f32
        ).reshape(2, CORES, width, BLK)
        for j in range(2):
            even, odd = part[j, 0], part[j, 1]
            to_even, to_odd = (place(2 * i + j, core) for core in range(CORES))
            keep_at = [jnp.where(mine, a, b) for a, b in zip(to_even, to_odd)]
            send_at = [jnp.where(mine, b, a) for a, b in zip(to_even, to_odd)]
            keep_ref[keep_at[0], keep_at[1]] = jnp.where(mine, even, odd)
            send_ref[send_at[0], send_at[1]] = jnp.where(mine, odd, even).astype(bf16)


def rotate_partials(ids, basis, own, lent):
    shape = (NEAR, FAR, own.shape[0], BLK)
    return pl.pallas_call(
        rotate_kernel,
        in_specs=[smem] + [vmem] * 5,
        out_specs=[vmem, vmem, smem],
        out_shape=[
            jax.ShapeDtypeStruct(shape, f32),
            jax.ShapeDtypeStruct(shape, bf16),
            jax.ShapeDtypeStruct((4,), jnp.int32),
        ],
        compiler_params=params,
    )(ids, basis, own, *lent)


def adam_moments(rotated, old_first, old_second):
    first = beta_first * old_first + (1.0 - beta_first) * rotated
    second = beta_second * old_second + (1.0 - beta_second) * rotated * rotated
    return first, second


def back_kernel(basis_ref, own_ref, other_ref, out_ref):
    width = basis_ref.shape[0]
    cols = 2 * CORES * width
    mine = lax.rem(lax.axis_index("hidden"), CORES) == 0
    total = jnp.zeros((width, BLK), f32)
    for i in range(XS * ZS // 2):
        pieces = []
        for j in range(2):
            even, odd = (place(2 * i + j, core) for core in range(CORES))
            pieces.append(jnp.where(mine, own_ref[even], other_ref[even]))
            pieces.append(jnp.where(mine, other_ref[odd], own_ref[odd]))
        total += jnp.dot(
            basis_ref[:, i * cols : (i + 1) * cols],
            jnp.concatenate(pieces, axis=0),
            preferred_element_type=f32,
        )
    out_ref[...] = total


def rotate_back(basis, own, other):
    return pl.pallas_call(
        back_kernel,
        in_specs=[vmem] * 3,
        out_specs=vmem,
        out_shape=jax.ShapeDtypeStruct((basis.shape[0], BLK), f32),
        compiler_params=params,
    )(basis, own, other)


def place(chip, core):
    x, z = (chip // ZS + core) % XS, (chip % ZS + core) % ZS
    return ((x + 1) // 2 % 2) * 2 + z % 2, (x // 2) * (ZS // 2) + z // 2


def groups():
    near = [[None] * NEAR for _ in range(CORES * FAR)]
    far = [[None] * FAR for _ in range(CORES * NEAR)]
    for chip in range(XS * ZS):
        for core in range(CORES):
            a, b = place(chip, core)
            near[core * FAR + b][a] = far[core * NEAR + a][b] = chip * CORES + core
    return near, far


NEAR_GROUPS, FAR_GROUPS = groups()


def all_to_all(x, members):
    return lax.all_to_all(x, "hidden", 0, 0, axis_index_groups=members, tiled=True)


def swap_cores(x):
    return lax.ppermute(x, "hidden", [(i, i ^ 1) for i in range(HIDDEN)])


def swap_owners_by(k, x):
    return lax.ppermute(x, "vocab", [(i, i ^ k) for i in range(OWNERS)])


def swap_owners(x):
    return [swap_owners_by(k, x) for k in (1, 2, 3)]


def swap_with_partner(match, x):
    return lax.switch(
        match - 1, [functools.partial(swap_owners_by, k) for k in range(1, OWNERS)], x
    )


def together(*x):
    return lax.optimization_barrier(x)


def shards(gradient, moment_first, moment_second, basis, block_ids):
    gradient, moment_first, moment_second = gradient.T, moment_first.T, moment_second.T
    ids = block_ids.T
    width = gradient.shape[0]

    def rows_of(table, block):
        return lax.dynamic_slice_in_dim(table, jnp.maximum(block, 0) * BLK, BLK, 1)

    lent_rows = swap_owners(gradient[:, BLK:])
    keep, send, roles = rotate_partials(ids, brought_near(basis), gradient[:, :BLK], lent_rows)
    match, own_ids = roles[MATCH], roles[ID_0 : ID_1 + 1]
    helping, doubled = roles[COUNT] == 0, roles[COUNT] == 2
    held_first = rows_of(moment_first, own_ids[1])
    held_second = rows_of(moment_second, own_ids[1])
    held = jnp.concatenate([held_first, held_second], axis=1)
    part = (keep + swap_cores(send).astype(f32)).astype(f16)
    lent = swap_with_partner(match, held)
    old_first = jnp.where(helping, lent[:, :BLK], rows_of(moment_first, own_ids[0]))
    old_second = jnp.where(helping, lent[:, BLK:], rows_of(moment_second, own_ids[0]))

    part = all_to_all(part, NEAR_GROUPS)
    part, old_first, old_second = together(part, old_first, old_second)
    part = all_to_all(jnp.sum(part.astype(f32), axis=0).astype(f16), FAR_GROUPS)
    rotated = jnp.sum(part.astype(f32), axis=0) * (1.0 / SCALE)

    first, second = adam_moments(rotated, old_first, old_second)
    direction = (first / (jnp.sqrt(second) + epsilon)).astype(bf16)
    gathered = all_to_all(jnp.broadcast_to(direction[None], (FAR, width, BLK)), FAR_GROUPS)
    other_rotated = swap_with_partner(match, rotated)
    first_1, second_1 = adam_moments(other_rotated, held_first, held_second)
    gathered, first_1, second_1, basis = together(gathered, first_1, second_1, basis)
    basis = brought_near(basis)
    gathered = jnp.broadcast_to(gathered[None], (NEAR, FAR, width, BLK))
    gathered = all_to_all(gathered, NEAR_GROUPS)

    def written(table, slot_0, slot_1):
        for block, live, new in ((own_ids[0], ~helping, slot_0), (own_ids[1], doubled, slot_1)):
            new = jnp.where(live, new, rows_of(table, block))
            table = lax.dynamic_update_slice_in_dim(table, new, jnp.maximum(block, 0) * BLK, 1)
        return table

    new_first = written(moment_first, first, first_1)
    new_second = written(moment_second, second, second_1)
    gathered, new_first, new_second = together(gathered, new_first, new_second)

    update = rotate_back(basis, gathered, swap_cores(gathered))
    lent_update = swap_with_partner(match, update)
    update = jnp.concatenate([update, lent_update], axis=1)
    second_half = lax.broadcasted_iota(jnp.int32, update.shape, 1) >= BLK
    update = jnp.where(jnp.where(second_half, doubled, ~helping), update, 0.0)
    return (update.T, new_first.T, new_second.T)


def solution(mesh):
    placed = P("vocab", "hidden")
    return jax.shard_map(
        shards,
        mesh=mesh,
        in_specs=(placed, placed, placed, P("hidden", None), P()),
        out_specs=(placed,) * 3,
        check_vma=False,
    )
```

```python
import functools

import jax
import jax.numpy as jnp
from jax import lax
from jax.experimental import pallas as pl
from jax.experimental.pallas import tpu as pltpu
from jax.sharding import PartitionSpec as P

BLK = 128
OWNERS = 4
XS, ZS, CORES = 4, 8, 2
HIDDEN = XS * ZS * CORES
NEAR, FAR = 4, 8
SCALE = 4.0
VMEM_LIMIT = 32 * 2**20
NEAR_LIMIT = 32 * 2**20

beta_first = 0.9
beta_second = 0.95
epsilon = 1e-08

f32, bf16, f16 = jnp.float32, jnp.bfloat16, jnp.float16

smem = pl.BlockSpec(memory_space=pltpu.SMEM)
vmem = pl.BlockSpec(memory_space=pltpu.VMEM)
anywhere = pl.BlockSpec(memory_space=pl.ANY)
params = pltpu.CompilerParams(vmem_limit_bytes=VMEM_LIMIT)

MATCH, COUNT, ID_0, ID_1 = range(4)


def live_slots(ids_ref, owner):
    return (ids_ref[0, owner] >= 0).astype(jnp.int32) + (ids_ref[1, owner] >= 0).astype(jnp.int32)


def matching(ids_ref):
    zero = live_slots(ids_ref, 0)
    return jnp.where(
        zero + live_slots(ids_ref, 1) == 2,
        1,
        jnp.where(zero + live_slots(ids_ref, 3) == 2, 3, 2),
    )


def pick(match, options):
    return jnp.where(match == 1, options[0], jnp.where(match == 2, options[1], options[2]))


def near_kernel(basis_ref, out_ref, sem):
    copy = pltpu.make_async_copy(basis_ref, out_ref, sem)
    copy.start()
    copy.wait()


def brought_near(basis):
    return pl.pallas_call(
        near_kernel,
        in_specs=[anywhere],
        out_specs=vmem,
        out_shape=jax.ShapeDtypeStruct(basis.shape, basis.dtype),
        scratch_shapes=[pltpu.SemaphoreType.DMA],
        compiler_params=pltpu.CompilerParams(vmem_limit_bytes=NEAR_LIMIT),
    )(basis)


def rotate_kernel(
    ids_ref, basis_ref, own_ref, one_ref, two_ref, three_ref, roles_ref, *refs
):
    keep_refs, send_refs, (keep_ref, send_ref) = refs[:NEAR], refs[NEAR : 2 * NEAR], refs[2 * NEAR :]
    width = own_ref.shape[0]
    cols = 2 * CORES * width
    me = lax.axis_index("vocab")
    match, count = matching(ids_ref), live_slots(ids_ref, me)
    roles_ref[MATCH], roles_ref[COUNT] = match, count
    roles_ref[ID_0], roles_ref[ID_1] = ids_ref[0, me], ids_ref[1, me]
    lent = pick(match, [one_ref[...], two_ref[...], three_ref[...]])
    rows = jnp.where(count == 0, lent, own_ref[...]) * jnp.bfloat16(SCALE)
    mine = lax.rem(lax.axis_index("hidden"), CORES) == 0
    members = [near_member(core) for core in range(CORES)]

    for i in range(XS * ZS // 2):
        at = pl.ds(i * cols, cols)
        part = lax.dot_general(
            basis_ref[:, at], rows, (((0,), (0,)), ((), ())), preferred_element_type=f32
        ).reshape(2, CORES, width, BLK)
        for j in range(2):
            even, odd = part[j, 0], part[j, 1]
            to_even, to_odd = (
                (place(2 * i + j, core)[0] ^ members[core], place(2 * i + j, core)[1])
                for core in range(CORES)
            )
            keep_at = [jnp.where(mine, a, b) for a, b in zip(to_even, to_odd)]
            send_at = [jnp.where(mine, b, a) for a, b in zip(to_even, to_odd)]
            keep_ref[keep_at[0], keep_at[1]] = jnp.where(mine, even, odd)
            send_ref[send_at[0], send_at[1]] = jnp.where(mine, odd, even).astype(bf16)
    for turn in range(NEAR):
        keep_refs[turn][...] = keep_ref[turn]
        send_refs[turn][...] = send_ref[turn]


def rotate_partials(ids, basis, own, lent):
    shape = (FAR, own.shape[0], BLK)
    out = pl.pallas_call(
        rotate_kernel,
        in_specs=[smem] + [vmem] * 5,
        out_specs=[smem] + [vmem] * (2 * NEAR),
        out_shape=[jax.ShapeDtypeStruct((4,), jnp.int32)]
        + [jax.ShapeDtypeStruct(shape, t) for t in (f32, bf16) for _ in range(NEAR)],
        scratch_shapes=[pltpu.VMEM((NEAR,) + shape, t) for t in (f32, bf16)],
        compiler_params=params,
    )(ids, basis, own, *lent)
    return out[0], out[1 : 1 + NEAR], out[1 + NEAR :]


def adam_moments(rotated, old_first, old_second):
    first = beta_first * old_first + (1.0 - beta_first) * rotated
    second = beta_second * old_second + (1.0 - beta_second) * rotated * rotated
    return first, second


def back_kernel(basis_ref, *refs):
    own_refs, other_refs, out_ref, cols_ref = refs[:NEAR], refs[NEAR : 2 * NEAR], refs[-2], refs[-1]
    width = basis_ref.shape[0]
    cols = 2 * CORES * width
    mine = lax.rem(lax.axis_index("hidden"), CORES) == 0
    for turn in range(NEAR):
        own, other = own_refs[turn][...], other_refs[turn][...]
        cols_ref[0, near_member(0) ^ turn] = jnp.where(mine, own, other)
        cols_ref[1, near_member(1) ^ turn] = jnp.where(mine, other, own)
    total = jnp.zeros((width, BLK), f32)
    for i in range(XS * ZS // 2):
        pieces = [
            cols_ref[(core,) + place(2 * i + j, core)] for j in range(2) for core in range(CORES)
        ]
        total += jnp.dot(
            basis_ref[:, i * cols : (i + 1) * cols],
            jnp.concatenate(pieces, axis=0),
            preferred_element_type=f32,
        )
    out_ref[...] = total


def rotate_back(basis, own, other):
    return pl.pallas_call(
        back_kernel,
        in_specs=[vmem] * (1 + 2 * NEAR),
        out_specs=vmem,
        out_shape=jax.ShapeDtypeStruct((basis.shape[0], BLK), f32),
        scratch_shapes=[pltpu.VMEM((CORES, NEAR, FAR, basis.shape[0], BLK), bf16)],
        compiler_params=params,
    )(basis, *own, *other)


def place(chip, core):
    x, z = (chip // ZS + core) % XS, (chip % ZS + core) % ZS
    return ((x + 1) // 2 % 2) * 2 + z % 2, (x // 2) * (ZS // 2) + z // 2


def near_member(core):
    at = lax.axis_index("hidden") // CORES
    x, z = lax.rem(at // ZS + core, XS), lax.rem(lax.rem(at, ZS) + core, ZS)
    return lax.rem((x + 1) // 2, 2) * 2 + lax.rem(z, 2)


def groups():
    near = [[None] * NEAR for _ in range(CORES * FAR)]
    far = [[None] * FAR for _ in range(CORES * NEAR)]
    for chip in range(XS * ZS):
        for core in range(CORES):
            a, b = place(chip, core)
            near[core * FAR + b][a] = far[core * NEAR + a][b] = chip * CORES + core
    return near, far


NEAR_GROUPS, FAR_GROUPS = groups()


def all_to_all(x, members):
    return lax.all_to_all(x, "hidden", 0, 0, axis_index_groups=members, tiled=True)


def near_by(x, turn):
    pairs = [(g[i], g[i ^ turn]) for g in NEAR_GROUPS for i in range(NEAR)]
    return lax.ppermute(x, "hidden", pairs)


def swap_cores(x):
    return lax.ppermute(x, "hidden", [(i, i ^ 1) for i in range(HIDDEN)])


def swap_owners_by(k, x):
    return lax.ppermute(x, "vocab", [(i, i ^ k) for i in range(OWNERS)])


def swap_owners(x):
    return [swap_owners_by(k, x) for k in (1, 2, 3)]


def swap_with_partner(match, x):
    return lax.switch(
        match - 1, [functools.partial(swap_owners_by, k) for k in range(1, OWNERS)], x
    )


def together(*x):
    return lax.optimization_barrier(x)


def shards(gradient, moment_first, moment_second, basis, block_ids):
    gradient, moment_first, moment_second = gradient.T, moment_first.T, moment_second.T
    ids = block_ids.T
    width = gradient.shape[0]

    def rows_of(table, block):
        at = (0, jnp.maximum(block, 0) * BLK)
        return lax.dynamic_slice(table, at, (width, BLK), allow_negative_indices=False)

    lent_rows = swap_owners(gradient[:, BLK:])
    roles, keep, send = rotate_partials(ids, brought_near(basis), gradient[:, :BLK], lent_rows)
    match, own_ids = roles[MATCH], roles[ID_0 : ID_1 + 1]
    helping, doubled = roles[COUNT] == 0, roles[COUNT] == 2
    held_first = rows_of(moment_first, own_ids[1])
    held_second = rows_of(moment_second, own_ids[1])
    held = jnp.concatenate([held_first, held_second], axis=1)
    order = (3, 1, 2, 0)
    got = {turn: swap_cores(send[turn]) for turn in order}
    part = {turn: keep[turn] + got[turn].astype(f32) for turn in order}
    total = part[0]
    for turn in order[:-1]:
        total = total + near_by(part[turn].astype(f16), turn).astype(f32)
    part, held = together(total.astype(f16), held)
    lent = swap_with_partner(match, held)
    old_first = jnp.where(helping, lent[:, :BLK], rows_of(moment_first, own_ids[0]))
    old_second = jnp.where(helping, lent[:, BLK:], rows_of(moment_second, own_ids[0]))

    part = all_to_all(part, FAR_GROUPS)
    rotated = jnp.sum(part.astype(f32), axis=0) * (1.0 / SCALE)

    first, second = adam_moments(rotated, old_first, old_second)
    direction = (first / (jnp.sqrt(second) + epsilon)).astype(bf16)
    gathered = all_to_all(jnp.broadcast_to(direction[None], (FAR, width, BLK)), FAR_GROUPS)
    other_rotated = swap_with_partner(match, rotated)
    first_1, second_1 = adam_moments(other_rotated, held_first, held_second)
    gathered, first, second, first_1, second_1, basis = together(
        gathered, first, second, first_1, second_1, basis
    )
    basis = brought_near(basis)
    own = [gathered] + [near_by(gathered, turn) for turn in range(1, NEAR)]

    def written(table, slot_0, slot_1):
        for block, live, new in ((own_ids[0], ~helping, slot_0), (own_ids[1], doubled, slot_1)):
            new = jnp.where(live, new, rows_of(table, block))
            at = (0, jnp.maximum(block, 0) * BLK)
            table = lax.dynamic_update_slice(table, new, at, allow_negative_indices=False)
        return table

    new_first = written(moment_first, first, first_1)
    new_second = written(moment_second, second, second_1)
    own[-1], new_first, new_second, basis = together(own[-1], new_first, new_second, basis)
    other = [swap_cores(x) for x in own]

    update = rotate_back(basis, own, other)
    lent_update = swap_with_partner(match, update.astype(f16))
    update = jnp.concatenate([update, lent_update.astype(f32)], axis=1)
    second_half = lax.broadcasted_iota(jnp.int32, update.shape, 1) >= BLK
    update = jnp.where(jnp.where(second_half, doubled, ~helping), update, 0.0)
    return (update.T, new_first.T, new_second.T)


def solution(mesh):
    placed = P("vocab", "hidden")
    return jax.shard_map(
        shards,
        mesh=mesh,
        in_specs=(placed, placed, placed, P("hidden", None), P()),
        out_specs=(placed,) * 3,
        check_vma=False,
    )
```

```python
import functools

import jax
import jax.numpy as jnp
from jax import lax
from jax.experimental import pallas as pl
from jax.experimental.pallas import tpu as pltpu
from jax.sharding import PartitionSpec as P

BLK = 128
OWNERS = 4
XS, ZS, CORES = 4, 8, 2
HIDDEN = XS * ZS * CORES
NEAR, FAR = 4, 8
NEAR_SCALE, FAR_SCALE = 128.0, 32.0
VMEM_LIMIT = 24 * 2**20
NEAR_LIMIT = 8 * 2**20

beta_first = 0.9
beta_second = 0.95
epsilon = 1e-08

f32, bf16, f16 = jnp.float32, jnp.bfloat16, jnp.float16

smem = pl.BlockSpec(memory_space=pltpu.SMEM)
vmem = pl.BlockSpec(memory_space=pltpu.VMEM)
anywhere = pl.BlockSpec(memory_space=pl.ANY)
params = pltpu.CompilerParams(vmem_limit_bytes=VMEM_LIMIT)

MATCH, COUNT, ID_0, ID_1 = range(4)


def live_slots(ids_ref, owner):
    return (ids_ref[0, owner] >= 0).astype(jnp.int32) + (ids_ref[1, owner] >= 0).astype(jnp.int32)


def matching(ids_ref):
    zero = live_slots(ids_ref, 0)
    return jnp.where(
        zero + live_slots(ids_ref, 1) == 2,
        1,
        jnp.where(zero + live_slots(ids_ref, 3) == 2, 3, 2),
    )


def pick(match, options):
    return jnp.where(match == 1, options[0], jnp.where(match == 2, options[1], options[2]))


def near_kernel(basis_ref, out_ref, sem):
    copy = pltpu.make_async_copy(basis_ref, out_ref, sem)
    copy.start()
    copy.wait()


def brought_near(basis):
    return pl.pallas_call(
        near_kernel,
        in_specs=[anywhere],
        out_specs=vmem,
        out_shape=jax.ShapeDtypeStruct(basis.shape, basis.dtype),
        scratch_shapes=[pltpu.SemaphoreType.DMA],
        compiler_params=pltpu.CompilerParams(vmem_limit_bytes=NEAR_LIMIT),
    )(basis)


def rotate_kernel(
    ids_ref, basis_ref, own_ref, one_ref, two_ref, three_ref, roles_ref, *refs
):
    keep_refs, send_refs, (keep_ref, send_ref) = refs[:NEAR], refs[NEAR : 2 * NEAR], refs[2 * NEAR :]
    width = own_ref.shape[0]
    cols = 2 * CORES * width
    me = lax.axis_index("vocab")
    match, count = matching(ids_ref), live_slots(ids_ref, me)
    roles_ref[MATCH], roles_ref[COUNT] = match, count
    roles_ref[ID_0], roles_ref[ID_1] = ids_ref[0, me], ids_ref[1, me]
    lent = pick(match, [one_ref[...], two_ref[...], three_ref[...]])
    rows = jnp.where(count == 0, lent, own_ref[:, :BLK]) * jnp.bfloat16(NEAR_SCALE)
    mine = lax.rem(lax.axis_index("hidden"), CORES) == 0
    members = [near_member(core) for core in range(CORES)]

    for i in range(XS * ZS // 2):
        at = pl.ds(i * cols, cols)
        part = lax.dot_general(
            basis_ref[:, at], rows, (((0,), (0,)), ((), ())), preferred_element_type=f32
        ).reshape(2, CORES, width, BLK)
        for j in range(2):
            even, odd = part[j, 0], part[j, 1]
            to_even, to_odd = (
                (place(2 * i + j, core)[0] ^ members[core], place(2 * i + j, core)[1])
                for core in range(CORES)
            )
            keep_at = [jnp.where(mine, a, b) for a, b in zip(to_even, to_odd)]
            send_at = [jnp.where(mine, b, a) for a, b in zip(to_even, to_odd)]
            keep_ref[keep_at[0], keep_at[1]] = jnp.where(mine, even, odd)
            send_ref[send_at[0], send_at[1]] = jnp.where(mine, odd, even).astype(bf16)
    for turn in range(NEAR):
        keep_refs[turn][...] = keep_ref[turn]
        send_refs[turn][...] = send_ref[turn]


def rotate_partials(ids, basis, own, lent):
    shape = (FAR, own.shape[0], BLK)
    out = pl.pallas_call(
        rotate_kernel,
        in_specs=[smem] + [vmem] * 5,
        out_specs=[smem] + [vmem] * (2 * NEAR),
        out_shape=[jax.ShapeDtypeStruct((4,), jnp.int32)]
        + [jax.ShapeDtypeStruct(shape, t) for t in (f32, bf16) for _ in range(NEAR)],
        scratch_shapes=[pltpu.VMEM((NEAR,) + shape, t) for t in (f32, bf16)],
        compiler_params=params,
    )(ids, basis, own, *lent)
    return out[0], out[1 : 1 + NEAR], out[1 + NEAR :]


def adam_moments(rotated, old_first, old_second):
    first = beta_first * old_first + (1.0 - beta_first) * rotated
    second = beta_second * old_second + (1.0 - beta_second) * rotated * rotated
    return first, second


def back_kernel(basis_ref, *refs):
    own_refs, other_refs, out_ref, cols_ref = refs[:NEAR], refs[NEAR : 2 * NEAR], refs[-2], refs[-1]
    width = basis_ref.shape[0]
    cols = 2 * CORES * width
    mine = lax.rem(lax.axis_index("hidden"), CORES) == 0
    for turn in range(NEAR):
        own, other = own_refs[turn][...], other_refs[turn][...]
        cols_ref[0, near_member(0) ^ turn] = jnp.where(mine, own, other)
        cols_ref[1, near_member(1) ^ turn] = jnp.where(mine, other, own)
    total = jnp.zeros((width, BLK), f32)
    for i in range(XS * ZS // 2):
        pieces = [
            cols_ref[(core,) + place(2 * i + j, core)] for j in range(2) for core in range(CORES)
        ]
        total += jnp.dot(
            basis_ref[:, i * cols : (i + 1) * cols],
            jnp.concatenate(pieces, axis=0),
            preferred_element_type=f32,
        )
    out_ref[...] = total


def rotate_back(basis, own, other):
    return pl.pallas_call(
        back_kernel,
        in_specs=[vmem] * (1 + 2 * NEAR),
        out_specs=vmem,
        out_shape=jax.ShapeDtypeStruct((basis.shape[0], BLK), f32),
        scratch_shapes=[pltpu.VMEM((CORES, NEAR, FAR, basis.shape[0], BLK), bf16)],
        compiler_params=params,
    )(basis, *own, *other)


def place(chip, core):
    x, z = (chip // ZS + core) % XS, (chip % ZS + core) % ZS
    return ((x + 1) // 2 % 2) * 2 + z % 2, (x // 2) * (ZS // 2) + z // 2


def near_member(core):
    at = lax.axis_index("hidden") // CORES
    x, z = lax.rem(at // ZS + core, XS), lax.rem(lax.rem(at, ZS) + core, ZS)
    return lax.rem((x + 1) // 2, 2) * 2 + lax.rem(z, 2)


def groups():
    near = [[None] * NEAR for _ in range(CORES * FAR)]
    far = [[None] * FAR for _ in range(CORES * NEAR)]
    for chip in range(XS * ZS):
        for core in range(CORES):
            a, b = place(chip, core)
            near[core * FAR + b][a] = far[core * NEAR + a][b] = chip * CORES + core
    return near, far


NEAR_GROUPS, FAR_GROUPS = groups()


def all_to_all(x, members):
    return lax.all_to_all(x, "hidden", 0, 0, axis_index_groups=members, tiled=True)


def near_by(x, turn):
    pairs = [(g[i], g[i ^ turn]) for g in NEAR_GROUPS for i in range(NEAR)]
    return lax.ppermute(x, "hidden", pairs)


def swap_cores(x):
    return lax.ppermute(x, "hidden", [(i, i ^ 1) for i in range(HIDDEN)])


def swap_owners_by(k, x):
    return lax.ppermute(x, "vocab", [(i, i ^ k) for i in range(OWNERS)])


def swap_owners(x):
    return [swap_owners_by(k, x) for k in (1, 2, 3)]


def swap_with_partner(match, x):
    return lax.switch(
        match - 1, [functools.partial(swap_owners_by, k) for k in range(1, OWNERS)], x
    )


def together(*x):
    return lax.optimization_barrier(x)


def shards(gradient, moment_first, moment_second, basis, block_ids):
    gradient, moment_first, moment_second = gradient.T, moment_first.T, moment_second.T
    ids = block_ids.T
    width = gradient.shape[0]

    def rows_of(table, block):
        at = (0, jnp.maximum(block, 0) * BLK)
        return lax.dynamic_slice(table, at, (width, BLK), allow_negative_indices=False)

    lent_rows = swap_owners(gradient[:, BLK:])
    roles, keep, send = rotate_partials(ids, brought_near(basis), gradient, lent_rows)
    match, own_ids = roles[MATCH], roles[ID_0 : ID_1 + 1]
    helping, doubled = roles[COUNT] == 0, roles[COUNT] == 2
    held_first = rows_of(moment_first, own_ids[1])
    held_second = rows_of(moment_second, own_ids[1])
    held = jnp.concatenate([held_first, held_second], axis=1)
    order = (3, 1, 2, 0)
    got = {turn: swap_cores(send[turn]) for turn in order}
    part = {turn: keep[turn] + got[turn].astype(f32) for turn in order}
    total = part[0]
    for turn in order[:-1]:
        total = total + near_by(part[turn].astype(f16), turn).astype(f32)
    part, held = together((total * (FAR_SCALE / NEAR_SCALE)).astype(f16), held)
    lent = swap_with_partner(match, held)
    old_first = jnp.where(helping, lent[:, :BLK], rows_of(moment_first, own_ids[0]))
    old_second = jnp.where(helping, lent[:, BLK:], rows_of(moment_second, own_ids[0]))

    part = all_to_all(part, FAR_GROUPS)
    rotated = jnp.sum(part.astype(f32), axis=0) * (1.0 / FAR_SCALE)

    first, second = adam_moments(rotated, old_first, old_second)
    direction = (first / (jnp.sqrt(second) + epsilon)).astype(bf16)
    gathered = all_to_all(jnp.broadcast_to(direction[None], (FAR, width, BLK)), FAR_GROUPS)
    other_rotated = swap_with_partner(match, rotated)
    first_1, second_1 = adam_moments(other_rotated, held_first, held_second)
    gathered, first, second, first_1, second_1, basis = together(
        gathered, first, second, first_1, second_1, basis
    )
    basis = brought_near(basis)
    own = [gathered] + [near_by(gathered, turn) for turn in range(1, NEAR)]

    def written(table, slot_0, slot_1):
        for block, live, new in ((own_ids[0], ~helping, slot_0), (own_ids[1], doubled, slot_1)):
            new = jnp.where(live, new, rows_of(table, block))
            at = (0, jnp.maximum(block, 0) * BLK)
            table = lax.dynamic_update_slice(table, new, at, allow_negative_indices=False)
        return table

    new_first = written(moment_first, first, first_1)
    new_second = written(moment_second, second, second_1)
    own[-1], new_first, new_second, basis = together(own[-1], new_first, new_second, basis)
    other = [swap_cores(x) for x in own]

    update = rotate_back(basis, own, other)
    lent_update = swap_with_partner(match, update.astype(f16))
    update = jnp.concatenate([update, lent_update.astype(f32)], axis=1)
    second_half = lax.broadcasted_iota(jnp.int32, update.shape, 1) >= BLK
    update = jnp.where(jnp.where(second_half, doubled, ~helping), update, 0.0)
    return (update.T, new_first.T, new_second.T)


def solution(mesh):
    placed = P("vocab", "hidden")
    return jax.shard_map(
        shards,
        mesh=mesh,
        in_specs=(placed, placed, placed, P("hidden", None), P()),
        out_specs=(placed,) * 3,
        check_vma=False,
    )
```

```python
import functools

import jax
import jax.numpy as jnp
from jax import lax
from jax.experimental import pallas as pl
from jax.experimental.pallas import tpu as pltpu
from jax.sharding import PartitionSpec as P

BLK = 128
OWNERS = 4
XS, ZS, CORES = 4, 8, 2
HIDDEN = XS * ZS * CORES
NEAR, FAR = 4, 8
NEAR_SCALE, FAR_SCALE = 128.0, 32.0
VMEM_LIMIT = 24 * 2**20
NEAR_LIMIT = 8 * 2**20

beta_first = 0.9
beta_second = 0.95
epsilon = 1e-08

f32, bf16, f16 = jnp.float32, jnp.bfloat16, jnp.float16

smem = pl.BlockSpec(memory_space=pltpu.SMEM)
vmem = pl.BlockSpec(memory_space=pltpu.VMEM)
anywhere = pl.BlockSpec(memory_space=pl.ANY)
params = pltpu.CompilerParams(vmem_limit_bytes=VMEM_LIMIT)

MATCH, COUNT, ID_0, ID_1 = range(4)


def live_slots(ids_ref, owner):
    return (ids_ref[0, owner] >= 0).astype(jnp.int32) + (ids_ref[1, owner] >= 0).astype(jnp.int32)


def matching(ids_ref):
    zero = live_slots(ids_ref, 0)
    return jnp.where(
        zero + live_slots(ids_ref, 1) == 2,
        1,
        jnp.where(zero + live_slots(ids_ref, 3) == 2, 3, 2),
    )


def pick(match, options):
    return jnp.where(match == 1, options[0], jnp.where(match == 2, options[1], options[2]))


def near_kernel(basis_ref, out_ref, sem):
    copy = pltpu.make_async_copy(basis_ref, out_ref, sem)
    copy.start()
    copy.wait()


def brought_near(basis):
    return pl.pallas_call(
        near_kernel,
        in_specs=[anywhere],
        out_specs=vmem,
        out_shape=jax.ShapeDtypeStruct(basis.shape, basis.dtype),
        scratch_shapes=[pltpu.SemaphoreType.DMA],
        compiler_params=pltpu.CompilerParams(vmem_limit_bytes=NEAR_LIMIT),
    )(basis)


def rotate_kernel(
    ids_ref, basis_ref, own_ref, one_ref, two_ref, three_ref, roles_ref, *refs
):
    keep_refs, send_refs, (keep_ref, send_ref) = refs[:NEAR], refs[NEAR : 2 * NEAR], refs[2 * NEAR :]
    width = own_ref.shape[0]
    cols = 2 * CORES * width
    me = lax.axis_index("vocab")
    match, count = matching(ids_ref), live_slots(ids_ref, me)
    roles_ref[MATCH], roles_ref[COUNT] = match, count
    roles_ref[ID_0], roles_ref[ID_1] = ids_ref[0, me], ids_ref[1, me]
    lent = pick(match, [one_ref[...], two_ref[...], three_ref[...]])
    rows = jnp.where(count == 0, lent, own_ref[:, :BLK]) * jnp.bfloat16(NEAR_SCALE)
    mine = lax.rem(lax.axis_index("hidden"), CORES) == 0
    members = [near_member(core) for core in range(CORES)]

    for i in range(XS * ZS // 2):
        at = pl.ds(i * cols, cols)
        part = lax.dot_general(
            basis_ref[:, at], rows, (((0,), (0,)), ((), ())), preferred_element_type=f32
        ).reshape(2, CORES, width, BLK)
        for j in range(2):
            even, odd = part[j, 0], part[j, 1]
            to_even, to_odd = (
                (place(2 * i + j, core)[0] ^ members[core], place(2 * i + j, core)[1])
                for core in range(CORES)
            )
            keep_at = [jnp.where(mine, a, b) for a, b in zip(to_even, to_odd)]
            send_at = [jnp.where(mine, b, a) for a, b in zip(to_even, to_odd)]
            keep_ref[keep_at[0], keep_at[1]] = jnp.where(mine, even, odd)
            send_ref[send_at[0], send_at[1]] = jnp.where(mine, odd, even).astype(bf16)
    for turn in range(NEAR):
        keep_refs[turn][...] = keep_ref[turn]
        send_refs[turn][...] = send_ref[turn]


def rotate_partials(ids, basis, own, lent):
    shape = (FAR, own.shape[0], BLK)
    out = pl.pallas_call(
        rotate_kernel,
        in_specs=[smem] + [vmem] * 5,
        out_specs=[smem] + [vmem] * (2 * NEAR),
        out_shape=[jax.ShapeDtypeStruct((4,), jnp.int32)]
        + [jax.ShapeDtypeStruct(shape, t) for t in (f32, bf16) for _ in range(NEAR)],
        scratch_shapes=[pltpu.VMEM((NEAR,) + shape, t) for t in (f32, bf16)],
        compiler_params=params,
    )(ids, basis, own, *lent)
    return out[0], out[1 : 1 + NEAR], out[1 + NEAR :]


def adam_moments(rotated, old_first, old_second):
    first = beta_first * old_first + (1.0 - beta_first) * rotated
    second = beta_second * old_second + (1.0 - beta_second) * rotated * rotated
    return first, second


def back_kernel(basis_ref, *refs):
    own_refs, other_refs, out_ref, cols_ref = refs[:NEAR], refs[NEAR : 2 * NEAR], refs[-2], refs[-1]
    width = basis_ref.shape[0]
    cols = 2 * CORES * width
    mine = lax.rem(lax.axis_index("hidden"), CORES) == 0
    for turn in range(NEAR):
        own, other = own_refs[turn][...], other_refs[turn][...]
        cols_ref[0, near_member(0) ^ turn] = jnp.where(mine, own, other)
        cols_ref[1, near_member(1) ^ turn] = jnp.where(mine, other, own)
    total = jnp.zeros((width, BLK), f32)
    for i in range(XS * ZS // 2):
        pieces = [
            cols_ref[(core,) + place(2 * i + j, core)] for j in range(2) for core in range(CORES)
        ]
        total += jnp.dot(
            basis_ref[:, i * cols : (i + 1) * cols],
            jnp.concatenate(pieces, axis=0),
            preferred_element_type=f32,
        )
    out_ref[...] = total


def rotate_back(basis, own, other):
    return pl.pallas_call(
        back_kernel,
        in_specs=[vmem] * (1 + 2 * NEAR),
        out_specs=vmem,
        out_shape=jax.ShapeDtypeStruct((basis.shape[0], BLK), f32),
        scratch_shapes=[pltpu.VMEM((CORES, NEAR, FAR, basis.shape[0], BLK), bf16)],
        compiler_params=params,
    )(basis, *own, *other)


def place(chip, core):
    x, z = (chip // ZS + core) % XS, (chip % ZS + core) % ZS
    return ((x + 1) // 2 % 2) * 2 + z % 2, (x // 2) * (ZS // 2) + z // 2


def near_member(core):
    at = lax.axis_index("hidden") // CORES
    x, z = lax.rem(at // ZS + core, XS), lax.rem(lax.rem(at, ZS) + core, ZS)
    return lax.rem((x + 1) // 2, 2) * 2 + lax.rem(z, 2)


def groups():
    near = [[None] * NEAR for _ in range(CORES * FAR)]
    far = [[None] * FAR for _ in range(CORES * NEAR)]
    for chip in range(XS * ZS):
        for core in range(CORES):
            a, b = place(chip, core)
            near[core * FAR + b][a] = far[core * NEAR + a][b] = chip * CORES + core
    return near, far


NEAR_GROUPS, FAR_GROUPS = groups()


def all_to_all(x, members):
    return lax.all_to_all(x, "hidden", 0, 0, axis_index_groups=members, tiled=True)


def near_by(x, turn):
    pairs = [(g[i], g[i ^ turn]) for g in NEAR_GROUPS for i in range(NEAR)]
    return lax.ppermute(x, "hidden", pairs)


def swap_cores(x):
    return lax.ppermute(x, "hidden", [(i, i ^ 1) for i in range(HIDDEN)])


def swap_owners_by(k, x):
    return lax.ppermute(x, "vocab", [(i, i ^ k) for i in range(OWNERS)])


def swap_owners(x):
    return [swap_owners_by(k, x) for k in (1, 2, 3)]


def swap_with_partner(match, x):
    return lax.switch(
        match - 1, [functools.partial(swap_owners_by, k) for k in range(1, OWNERS)], x
    )


def together(*x):
    return lax.optimization_barrier(x)


def shards(gradient, moment_first, moment_second, basis, block_ids):
    gradient, moment_first, moment_second = gradient.T, moment_first.T, moment_second.T
    ids = block_ids.T
    width = gradient.shape[0]

    def rows_of(table, block):
        at = (0, jnp.maximum(block, 0) * BLK)
        return lax.dynamic_slice(table, at, (width, BLK), allow_negative_indices=False)

    lent_rows = swap_owners(gradient[:, BLK:])
    roles, keep, send = rotate_partials(ids, brought_near(basis), gradient, lent_rows)
    match, own_ids = roles[MATCH], roles[ID_0 : ID_1 + 1]
    helping, doubled = roles[COUNT] == 0, roles[COUNT] == 2
    held_first = rows_of(moment_first, own_ids[1])
    held_second = rows_of(moment_second, own_ids[1])
    held = jnp.concatenate([held_first, held_second], axis=1)
    order = (3, 1, 2, 0)
    got = {turn: swap_cores(send[turn]) for turn in order}
    part = {turn: keep[turn] + got[turn].astype(f32) for turn in order}
    total = part[0]
    for turn in order[:-1]:
        total = total + near_by(part[turn].astype(f16), turn).astype(f32)
    part, held = together((total * (FAR_SCALE / NEAR_SCALE)).astype(f16), held)
    lent = swap_with_partner(match, held)
    old_first = jnp.where(helping, lent[:, :BLK], rows_of(moment_first, own_ids[0]))
    old_second = jnp.where(helping, lent[:, BLK:], rows_of(moment_second, own_ids[0]))

    part = all_to_all(part, FAR_GROUPS)
    rotated = jnp.sum(part.astype(f32), axis=0) * (1.0 / FAR_SCALE)

    first, second = adam_moments(rotated, old_first, old_second)
    direction = (first / (jnp.sqrt(second) + epsilon)).astype(bf16)
    gathered = all_to_all(jnp.broadcast_to(direction[None], (FAR, width, BLK)), FAR_GROUPS)
    other_rotated = swap_with_partner(match, rotated)
    first_1, second_1 = adam_moments(other_rotated, held_first, held_second)
    gathered, first, second, first_1, second_1, basis = together(
        gathered, first, second, first_1, second_1, basis
    )
    basis = brought_near(basis)
    own = [gathered] + [near_by(gathered, turn) for turn in range(1, NEAR)]

    def written(table, slot_0, slot_1):
        for block, live, new in ((own_ids[0], ~helping, slot_0), (own_ids[1], doubled, slot_1)):
            new = jnp.where(live, new, rows_of(table, block))
            at = (0, jnp.maximum(block, 0) * BLK)
            table = lax.dynamic_update_slice(table, new, at, allow_negative_indices=False)
        return table

    new_first = written(moment_first, first, first_1)
    new_second = written(moment_second, second, second_1)
    own[-1], new_first, new_second, basis = together(own[-1], new_first, new_second, basis)
    other = [swap_cores(x) for x in own]

    update = rotate_back(basis, own, other)
    lent_update = swap_with_partner(match, update.astype(f16))
    update = jnp.pad(update, ((0, 0), (0, BLK)))
    lent_update = jnp.pad(lent_update, ((0, 0), (BLK, 0)))
    second_half = lax.broadcasted_iota(jnp.int32, update.shape, 1) >= BLK
    update = jnp.where(
        second_half,
        jnp.where(doubled, lent_update.astype(f32), 0.0),
        jnp.where(helping, 0.0, update),
    )
    return (update.T, new_first.T, new_second.T)


def solution(mesh):
    placed = P("vocab", "hidden")
    return jax.shard_map(
        shards,
        mesh=mesh,
        in_specs=(placed, placed, placed, P("hidden", None), P()),
        out_specs=(placed,) * 3,
        check_vma=False,
    )
```
